256 devices in a mesh: wide: 16 (over z_lo, x), narrow: 16 (over y, z_hi, core).
Axes of the slice: x: 4, y: 4, z: 8 (z_hi: 2, z_lo: 4; z = z_hi * 4 + z_lo), core: 2. Of those that a mesh axis runs over, the one named last changes fastest.
Arguments:
- residual: bfloat16 [1024, 8192], P('narrow', 'wide'), may hold values from -40 to 40
- queries: bfloat16 [1024, 8192], P('wide', 'narrow'), may hold values from -500 to 500
- key_cache: bfloat16 [32, 1024, 1024], P('wide', 'narrow'), may hold values from -7 to 7
- value_cache: bfloat16 [32, 1024, 1024], P('wide', 'narrow'), may hold values from -6 to 6
- out_proj: bfloat16 [8192, 8192], P('narrow', 'wide'), may hold values from -0.5 to 0.5
- norm_gain: bfloat16 [8192], P('wide'), may hold values from 0.099609375 to 1.8984375
- gate_proj: bfloat16 [8192, 28672], P('wide', 'narrow'), may hold values from -0.0625 to 0.0625
- up_proj: bfloat16 [8192, 28672], P('wide', 'narrow'), may hold values from -0.0625 to 0.0625
- down_proj: bfloat16 [28672, 8192], P('narrow', 'wide'), may hold values from -0.03125 to 0.03125
- example_ids: int32 [32], replicated, may hold values from 0 to 999999
- sample_ids: int32 [32], replicated, may hold values from 0 to 15
- layer_index: int32 [1], replicated, may hold values from 0 to 79
- dropout_seed: int32 [2], replicated, may hold values from 0 to 16777215
Outputs:
- layer_out: bfloat16 [1024, 8192], P('narrow', 'wide')
The draws below stay inside these ranges and needn't reach their ends.
All inputs are finite; a program needn't handle non-finite values.
Results may differ from the reference program's by a relative error of at most 0.02.
Values may be sent and summed in bfloat16 or wider, within the bound.
No kernel may reach another device: no remote copies, remote signals or barrier semaphores. Data moves between devices by JAX's collectives and lax.ppermute only.
A program may use at most 128 MiB of HBM per device.

```python
import math
import jax
import jax.numpy as jnp
from jax import lax

MODEL_WIDTH = 8192
FFN_WIDTH = 28672
HEADS = 64
KV_HEADS = 8
HEAD_DIM = 128
CTX = 1024
WIN = 32
SEQS = 32
TOKENS = 1024
N_WIDE = 16
N_NARROW = 16


def shared_keys(key):
    noise_base = jax.random.normal(jax.random.fold_in(key, 7), (SEQS, CTX, KV_HEADS, HEAD_DIM), jnp.float32)
    return jnp.clip(noise_base, -6.0, 6.0)


def draw_key_cache(key, part):
    keys_base = shared_keys(key)
    return keys_base.reshape(SEQS, CTX, KV_HEADS * HEAD_DIM).astype(jnp.bfloat16)


def draw_queries(key, part):
    fresh = 1.2 * jnp.clip(jax.random.normal(jax.random.fold_in(key, 9), (TOKENS, HEADS, HEAD_DIM), jnp.float32), -6.0, 6.0)
    return fresh.reshape(TOKENS, HEADS * HEAD_DIM).astype(jnp.bfloat16)


def draw_residual(key, part):
    base_key, row_key, col_key = jax.random.split(jax.random.fold_in(key, 11), 3)
    noise_base = jnp.clip(jax.random.normal(base_key, (TOKENS, MODEL_WIDTH), jnp.float32), -3.0, 3.0)
    row_scale = jnp.exp(jax.random.uniform(row_key, (TOKENS, 1), jnp.float32, math.log(0.3), math.log(3.0)))
    column = jnp.arange(MODEL_WIDTH, dtype=jnp.float32)
    column_rise = 0.3 * jnp.exp(column * (math.log(10.0) / MODEL_WIDTH))
    jitter = jnp.exp(jax.random.uniform(col_key, (MODEL_WIDTH,), jnp.float32, -0.35, 0.35))
    return (noise_base * row_scale * (column_rise * jitter)[None, :]).astype(jnp.bfloat16)


def set_ends(values, key, low, top_value):
    spot = [jax.random.randint(jax.random.fold_in(key, axis), (), 0, length) for axis, length in enumerate(values.shape)]
    main_axis = values.shape.index(max(values.shape))
    next_to = spot[:main_axis] + [(spot[main_axis] + 1) % values.shape[main_axis]] + spot[main_axis + 1:]
    return values.at[tuple(spot)].set(low).at[tuple(next_to)].set(top_value)


def level_of(stream_key, extent, shards, low, top_value):
    def one(dim, blocks):
        draws = jax.random.uniform(jax.random.fold_in(jax.random.fold_in(stream_key, 6), dim), (blocks,), jnp.float32, low / len(shards), top_value / len(shards))
        return jnp.repeat(jnp.exp(draws), extent[dim] // blocks).reshape((-1,) + (1,) * (len(extent) - dim - 1))

    level = one(*shards[0])
    for cut in shards[1:]:
        level = level * one(*cut)
    return level


def centred(stream_key, shape, width, bound, shards=(), kind=jnp.bfloat16):
    factor_of = level_of(stream_key, shape, shards, -0.22, 0.18) if shards else 1.0
    entries = jax.random.normal(stream_key, shape, jnp.float32) * width * factor_of
    return jnp.minimum(jnp.maximum(entries, -bound), bound).astype(kind)


def setup_inputs(seed: int = 0) -> dict:
    key_list = jax.random.split(jax.random.key(seed), 14)
    residual = draw_residual(jax.random.fold_in(key_list[13], 71), 0)
    queries = draw_queries(jax.random.fold_in(key_list[13], 71), 0)
    key_cache = draw_key_cache(jax.random.fold_in(key_list[13], 71), 0)
    value_cache = centred(key_list[3], (SEQS, CTX, KV_HEADS * HEAD_DIM), 1.0, 6.0, ((0, 16), (1, 16)))
    out_proj = centred(key_list[4], (HEADS * HEAD_DIM, MODEL_WIDTH), (HEADS * HEAD_DIM // 64) ** -0.5, 0.5, ((0, 16), (1, 16)))
    norm_gain = jnp.clip(1.0 + 0.18 * jax.random.normal(key_list[5], (MODEL_WIDTH,), jnp.float32), 0.099609375, 1.8984375).astype(jnp.bfloat16)
    gate_proj = centred(key_list[6], (MODEL_WIDTH, FFN_WIDTH), MODEL_WIDTH ** -0.5, 0.0625, ((0, 16), (1, 16)))
    up_proj = centred(key_list[7], (MODEL_WIDTH, FFN_WIDTH), MODEL_WIDTH ** -0.5, 0.0625, ((0, 16), (1, 16)))
    down_proj = centred(key_list[8], (FFN_WIDTH, MODEL_WIDTH), FFN_WIDTH ** -0.5, 0.03125, ((0, 16), (1, 16)))
    example_ids = set_ends(jax.random.randint(key_list[9], (SEQS,), 0, 1000000), jax.random.fold_in(key_list[9], 1), 0, 999999).astype(jnp.int32)
    sample_ids = set_ends(jax.random.randint(key_list[10], (SEQS,), 0, 16), jax.random.fold_in(key_list[10], 1), 0, 15).astype(jnp.int32)
    layer_index = jax.random.randint(key_list[11], (1,), 0, 80).astype(jnp.int32)
    dropout_seed = jax.random.randint(key_list[12], (2,), 0, 16777216).astype(jnp.int32)
    return dict(residual=residual, queries=queries, key_cache=key_cache, value_cache=value_cache, out_proj=out_proj, norm_gain=norm_gain, gate_proj=gate_proj, up_proj=up_proj, down_proj=down_proj, example_ids=example_ids, sample_ids=sample_ids, layer_index=layer_index, dropout_seed=dropout_seed)


drop_cut = 6554
keep_scale = 1.0 / 0.9
epsilon = 1e-05
neg_fill = -1e+30

def mix_bits(word_bits):
    word_bits = word_bits ^ lax.shift_right_logical(word_bits, jnp.int32(16))
    word_bits = word_bits * 2146121005
    word_bits = word_bits ^ lax.shift_right_logical(word_bits, jnp.int32(15))
    word_bits = word_bits * 1147971211
    word_bits = word_bits ^ lax.shift_right_logical(word_bits, jnp.int32(16))
    return word_bits

def pick_rows(id_table, seq_index):
    matches = seq_index[:, None] == jnp.arange(id_table.shape[0], dtype=jnp.int32)[None, :]
    return lax.optimization_barrier(jnp.sum(jnp.where(matches, id_table[None, :], 0), axis=1)).astype(jnp.int32)

def keep_factor(token_index, column_index, example_ids, sample_ids, layer_index, dropout_seed, stream_tag):
    seq_index = token_index // WIN
    position = token_index % WIN + (CTX - WIN)
    row_bits = mix_bits(dropout_seed[1] ^ position)
    row_bits = mix_bits(row_bits ^ layer_index[0] * 2 + stream_tag)
    row_bits = mix_bits(row_bits ^ pick_rows(sample_ids, seq_index))
    row_bits = mix_bits(row_bits ^ pick_rows(example_ids, seq_index))
    row_bits = mix_bits(row_bits ^ dropout_seed[0])
    cell_bits = mix_bits(row_bits[:, None] ^ column_index[None, :] * 1640531527)
    return jnp.where(cell_bits & 65535 >= drop_cut, keep_scale, 0.0).astype(jnp.float32)

def attend_one(operands):
    query_seq, key_seq, value_seq = operands
    group_size = HEADS // KV_HEADS
    query_blocks = query_seq.astype(jnp.float32).reshape(WIN, KV_HEADS, group_size, HEAD_DIM)
    key_blocks = key_seq.astype(jnp.float32).reshape(CTX, KV_HEADS, HEAD_DIM)
    value_blocks = value_seq.astype(jnp.float32).reshape(CTX, KV_HEADS, HEAD_DIM)
    scores = jnp.einsum('wkgd,ckd->wkgc', query_blocks, key_blocks) * (1.0 / math.sqrt(HEAD_DIM))
    key_position = jnp.arange(CTX, dtype=jnp.int32)
    query_position = CTX - WIN + jnp.arange(WIN, dtype=jnp.int32)
    visible = (key_position[None, :] <= query_position[:, None])[:, None, None, :]
    masked = jnp.where(visible, scores, neg_fill)
    row_max = lax.optimization_barrier(jnp.max(masked, axis=-1, keepdims=True))
    weights = jnp.where(visible, jnp.exp(masked - row_max), 0.0)
    totals = lax.optimization_barrier(jnp.sum(weights, axis=-1))
    rounded = lax.optimization_barrier(weights.astype(jnp.bfloat16)).astype(jnp.float32)
    numerator = jnp.einsum('wkgc,ckd->wkgd', rounded, value_blocks)
    attended = (numerator / totals[..., None]).astype(jnp.bfloat16)
    return attended.reshape(WIN, HEADS * HEAD_DIM)

def reference(residual, queries, key_cache, value_cache, out_proj, norm_gain, gate_proj, up_proj, down_proj, example_ids, sample_ids, layer_index, dropout_seed):
    attended = lax.map(attend_one, (queries.reshape(SEQS, WIN, HEADS * HEAD_DIM), key_cache, value_cache))
    attended = attended.reshape(TOKENS, HEADS * HEAD_DIM)
    group_width = HEADS * HEAD_DIM // N_NARROW
    att_groups = attended.reshape(TOKENS, N_NARROW, group_width).transpose(1, 0, 2)
    proj_groups = out_proj.reshape(N_NARROW, group_width, MODEL_WIDTH)

    def add_group(running, operands):
        att_part, proj_part = operands
        group_term = jnp.dot(att_part, proj_part, preferred_element_type=jnp.float32)
        return (running + lax.optimization_barrier(group_term.astype(jnp.bfloat16)).astype(jnp.float32), None)
    branch_term, _ = lax.scan(add_group, jnp.zeros((TOKENS, MODEL_WIDTH), jnp.float32), (att_groups, proj_groups))
    token_index = jnp.arange(TOKENS, dtype=jnp.int32)
    column_index = jnp.arange(MODEL_WIDTH, dtype=jnp.int32)
    keep_first = keep_factor(token_index, column_index, example_ids, sample_ids, layer_index, dropout_seed, 0)
    stream = (residual.astype(jnp.float32) + keep_first * branch_term).astype(jnp.bfloat16)
    stream_float = stream.astype(jnp.float32)
    inverse_rms = lax.rsqrt(lax.optimization_barrier(jnp.sum(stream_float * stream_float, axis=1)) / MODEL_WIDTH + epsilon)
    normed = (stream_float * inverse_rms[:, None] * norm_gain.astype(jnp.float32)[None, :]).astype(jnp.bfloat16)
    block_width = MODEL_WIDTH // N_WIDE
    normed_blocks = normed.reshape(TOKENS, N_WIDE, block_width).transpose(1, 0, 2)
    gate_blocks = gate_proj.reshape(N_WIDE, block_width, FFN_WIDTH)
    up_blocks = up_proj.reshape(N_WIDE, block_width, FFN_WIDTH)

    def add_block(running, operands):
        normed_part, gate_part, up_part = operands
        gate_term = jnp.dot(normed_part, gate_part, preferred_element_type=jnp.float32)
        up_term = jnp.dot(normed_part, up_part, preferred_element_type=jnp.float32)
        gate_term = lax.optimization_barrier(gate_term.astype(jnp.bfloat16)).astype(jnp.float32)
        up_term = lax.optimization_barrier(up_term.astype(jnp.bfloat16)).astype(jnp.float32)
        return ((running[0] + gate_term, running[1] + up_term), None)
    zero_rows = jnp.zeros((TOKENS, FFN_WIDTH), jnp.float32)
    (gate_sum, up_sum), _ = lax.scan(add_block, (zero_rows, zero_rows), (normed_blocks, gate_blocks, up_blocks))
    hidden = (jax.nn.silu(gate_sum) * up_sum).astype(jnp.bfloat16)
    ffn_term = jnp.dot(hidden, down_proj, preferred_element_type=jnp.float32)
    keep_second = keep_factor(token_index, column_index, example_ids, sample_ids, layer_index, dropout_seed, 1)
    return (stream_float + keep_second * ffn_term).astype(jnp.bfloat16)
```

```python
import math

import jax
import jax.numpy as jnp
from jax import lax
from jax.sharding import Mesh, PartitionSpec as P

MODEL_WIDTH = 8192
KV_HEADS = 8
GROUP = 8
HEAD_DIM = 128
CTX = 1024
WIN = 32
AXES = ("zl", "x", "y", "zh", "c")
WIDE = ("zl", "x")
NARROW = ("y", "zh", "c")

drop_cut = 6554
keep_scale = 1.0 / 0.9
epsilon = 1e-05
neg_fill = -1e30
f32 = jnp.float32
bf16 = jnp.bfloat16


def mix_bits(word_bits):
    word_bits = word_bits ^ lax.shift_right_logical(word_bits, jnp.int32(16))
    word_bits = word_bits * 2146121005
    word_bits = word_bits ^ lax.shift_right_logical(word_bits, jnp.int32(15))
    word_bits = word_bits * 1147971211
    word_bits = word_bits ^ lax.shift_right_logical(word_bits, jnp.int32(16))
    return word_bits


def pick_rows(id_table, seq_index):
    matches = seq_index[:, None] == jnp.arange(id_table.shape[0], dtype=jnp.int32)[None, :]
    return jnp.sum(jnp.where(matches, id_table[None, :], 0), axis=1)


def keep_factor(
    token_index, column_index, example_ids, sample_ids, layer_index, dropout_seed, stream_tag
):
    seq_index = token_index // WIN
    position = token_index % WIN + (CTX - WIN)
    row_bits = mix_bits(dropout_seed[1] ^ position)
    row_bits = mix_bits(row_bits ^ layer_index[0] * 2 + stream_tag)
    row_bits = mix_bits(row_bits ^ pick_rows(sample_ids, seq_index))
    row_bits = mix_bits(row_bits ^ pick_rows(example_ids, seq_index))
    row_bits = mix_bits(row_bits ^ dropout_seed[0])
    cell_bits = mix_bits(row_bits[:, None] ^ column_index[None, :] * 1640531527)
    return jnp.where(cell_bits & 65535 >= drop_cut, keep_scale, 0.0).astype(f32)


def shift(value, axis, step):
    n = lax.axis_size(axis)
    return lax.ppermute(value, axis, [(i, (i + step) % n) for i in range(n)])


def spread(value, axis):
    n = lax.axis_size(axis)
    return lax.all_to_all(
        jnp.broadcast_to(value[None], (n,) + value.shape), axis, 0, 0, tiled=True
    )


def pair_swap(rows, core):
    kept = lax.dynamic_index_in_dim(rows, core, 0, keepdims=False)
    given = lax.dynamic_index_in_dim(rows, 1 - core, 0, keepdims=False)
    got = shift(given, "c", 1)
    first = core == 0
    return jnp.stack([jnp.where(first, kept, got), jnp.where(first, got, kept)])


def on_device(
    residual,
    queries,
    key_cache,
    value_cache,
    out_proj,
    norm_gain,
    gate_proj,
    up_proj,
    down_proj,
    example_ids,
    sample_ids,
    layer_index,
    dropout_seed,
):
    zl, x, y, zh, c = (lax.axis_index(a) for a in AXES)
    nx, nz = lax.axis_size("x"), lax.axis_size("zl")
    chip = y * lax.axis_size("zh") + zh
    quarter = gate_proj.shape[1] // nx

    local_ctx = key_cache.shape[1]

    def by_owner(cache):
        return cache.reshape(2, local_ctx, KV_HEADS, HEAD_DIM).transpose(2, 0, 1, 3)

    cache_send = jnp.stack([by_owner(key_cache), by_owner(value_cache)], axis=2)
    cache_send = cache_send.reshape(2 * KV_HEADS, 2, local_ctx, HEAD_DIM)
    cache_got = lax.all_to_all(cache_send, NARROW, 0, 0, tiled=True)
    keys = cache_got[:, 0].reshape(CTX, HEAD_DIM)
    values = cache_got[:, 1].reshape(CTX, HEAD_DIM)

    q_seqs = queries.reshape(2, WIN, -1)
    q_own = lax.dynamic_index_in_dim(q_seqs, c, 0, keepdims=False)
    q_other = shift(lax.dynamic_index_in_dim(q_seqs, 1 - c, 0, keepdims=False), "c", 1)
    q_all = jnp.concatenate([q_own, q_other], axis=1).reshape(WIN * GROUP, HEAD_DIM)
    out_other = shift(out_proj, "c", 1)
    gain_blocks = [norm_gain] + [shift(norm_gain, "x", k) for k in range(1, nx)]

    def gate_up_piece(k):
        at = (x + k) % nx * quarter
        return jnp.concatenate(
            [
                lax.dynamic_slice_in_dim(gate_proj, at, quarter, 1),
                lax.dynamic_slice_in_dim(up_proj, at, quarter, 1),
            ],
            axis=1,
        )

    def down_piece(k):
        return lax.dynamic_slice_in_dim(down_proj, (x + k) % nx * quarter, quarter, 0)

    gate_up_own = [gate_up_piece(0)] + [shift(gate_up_piece(k), "x", k) for k in range(1, nx)]
    gate_up_pair = [shift(w, "c", 1) for w in gate_up_own]

    scores = lax.dot_general(
        q_all, keys, (((1,), (1,)), ((), ())), preferred_element_type=f32
    ) * (1.0 / math.sqrt(HEAD_DIM))
    row_position = CTX - WIN + jnp.arange(WIN * GROUP, dtype=jnp.int32) // GROUP
    visible = jnp.arange(CTX, dtype=jnp.int32)[None, :] <= row_position[:, None]
    masked = jnp.where(visible, scores, neg_fill)
    weights = jnp.where(visible, jnp.exp(masked - jnp.max(masked, axis=1, keepdims=True)), 0.0)
    totals = jnp.sum(weights, axis=1, keepdims=True)
    attended = jnp.dot(weights.astype(bf16), values, preferred_element_type=f32) / totals
    attended = attended.astype(bf16).reshape(WIN, GROUP * HEAD_DIM)

    att = spread(attended, "zl")
    att = spread(att, "x").transpose(1, 0, 2, 3).reshape(-1, GROUP * HEAD_DIM)
    half = out_proj.shape[0]
    attn_terms = jnp.dot(att[:, :half], out_proj, preferred_element_type=f32) + jnp.dot(
        att[:, half:], out_other, preferred_element_type=f32
    )
    attn_terms = attn_terms.astype(bf16)
    down_proj, attn_terms = lax.optimization_barrier((down_proj, attn_terms))
    down_own = [down_piece(0)] + [shift(down_piece(k), "x", k) for k in range(1, nx)]
    down_pair = [shift(w, "c", 1) for w in down_own]

    own_rows, width = residual.shape
    n_chips = lax.axis_size("y") * lax.axis_size("zh")

    def sum_chips(terms):
        got = lax.all_to_all(
            terms.reshape(n_chips, own_rows, width), ("y", "zh"), 0, 0, tiled=True
        )
        return jnp.sum(got.astype(f32), axis=0)

    attn_share = sum_chips(attn_terms)
    column_index = (zl * nx + x) * width + jnp.arange(width, dtype=jnp.int32)
    row = jnp.arange(own_rows, dtype=jnp.int32)
    tokens = (4 * chip + c + 2 * (row // WIN)) * WIN + row % WIN
    keep_args = (tokens, column_index, example_ids, sample_ids, layer_index, dropout_seed)
    residual_here = pair_swap(residual.reshape(2, WIN, width), c).reshape(own_rows, width)
    stream = (residual_here.astype(f32) + keep_factor(*keep_args, 0) * attn_share).astype(bf16)

    other = shift(stream, "zh", 1)
    lower = zh == 0
    rows2 = jnp.stack([jnp.where(lower, stream, other), jnp.where(lower, other, stream)])
    rows_all = spread(rows2, "y").reshape(n_chips * own_rows, width)
    stream_blocks = [rows_all] + [shift(rows_all, "x", k) for k in range(1, nx)]
    squares = sum(jnp.sum(jnp.square(b.astype(f32)), axis=1) for b in stream_blocks)
    scaled = [
        (b.astype(f32) * g.astype(f32)[None, :]).astype(bf16)
        for b, g in zip(stream_blocks, gain_blocks)
    ]
    part_rows = n_chips * own_rows // nz

    def gate_up_rows(k):
        at = (zl + k) % nz * part_rows
        own = pair = 0.0
        for b, w, v in zip(scaled, gate_up_own, gate_up_pair):
            b = lax.dynamic_slice_in_dim(b, at, part_rows, 0)
            own = own + jnp.dot(b, w, preferred_element_type=f32)
            pair = pair + jnp.dot(b, v, preferred_element_type=f32)
        sq = lax.dynamic_slice_in_dim(squares, at, part_rows, 0)
        return own.astype(bf16), pair.astype(bf16), sq

    own_sum = pair_sum = square_sum = 0.0
    for k in (2, 1, 3, 0):
        own, pair, sq = gate_up_rows(k)
        if k:
            own, pair, sq = shift(own, "zl", k), shift(pair, "zl", k), shift(sq, "zl", k)
        own_sum = own_sum + own.astype(f32)
        pair_sum = pair_sum + pair.astype(f32)
        square_sum = square_sum + sq
    inverse_rms = lax.rsqrt(square_sum / MODEL_WIDTH + epsilon)[:, None]

    def gated(both):
        both = both * inverse_rms
        return (jax.nn.silu(both[:, :quarter]) * both[:, quarter:]).astype(bf16)

    hidden = jnp.concatenate([gated(own_sum), gated(pair_sum)], axis=1)
    hidden = spread(hidden, "zl").reshape(n_chips * own_rows, 2 * quarter)

    def ffn_block(k):
        return jnp.dot(hidden[:, :quarter], down_own[k], preferred_element_type=f32) + jnp.dot(
            hidden[:, quarter:], down_pair[k], preferred_element_type=f32
        )

    ffn_terms = 0.0
    for k in (2, 1, 3, 0):
        term = ffn_block(k)
        if k:
            term = shift(term.astype(bf16), "x", -k).astype(f32)
        ffn_terms = ffn_terms + term
    ffn_share = sum_chips(ffn_terms.astype(bf16))
    layer_out = (stream.astype(f32) + keep_factor(*keep_args, 1) * ffn_share).astype(bf16)
    return pair_swap(layer_out.reshape(2, WIN, width), c).reshape(own_rows, width)


def solution(mesh):
    fine = Mesh(mesh.devices.reshape(4, 4, 4, 2, 2), AXES)
    return jax.shard_map(
        on_device,
        mesh=fine,
        in_specs=(
            P(NARROW, WIDE),
            P(WIDE, NARROW),
            P(WIDE, NARROW, None),
            P(WIDE, NARROW, None),
            P(NARROW, WIDE),
            P(WIDE),
            P(WIDE, NARROW),
            P(WIDE, NARROW),
            P(NARROW, WIDE),
            P(),
            P(),
            P(),
            P(),
        ),
        out_specs=P(NARROW, WIDE),
        check_vma=False,
    )
```

```python
import math

import jax
import jax.numpy as jnp
from jax import lax
from jax.sharding import Mesh, PartitionSpec as P

MODEL_WIDTH = 8192
KV_HEADS = 8
GROUP = 8
HEAD_DIM = 128
CTX = 1024
WIN = 32
AXES = ("zl", "x", "y", "zh", "c")
WIDE = ("zl", "x")
NARROW = ("y", "zh", "c")

drop_cut = 6554
keep_scale = 1.0 / 0.9
epsilon = 1e-05
neg_fill = -1e30
f32 = jnp.float32
bf16 = jnp.bfloat16


def mix_bits(word_bits):
    word_bits = word_bits ^ lax.shift_right_logical(word_bits, jnp.int32(16))
    word_bits = word_bits * 2146121005
    word_bits = word_bits ^ lax.shift_right_logical(word_bits, jnp.int32(15))
    word_bits = word_bits * 1147971211
    word_bits = word_bits ^ lax.shift_right_logical(word_bits, jnp.int32(16))
    return word_bits


def pick_rows(id_table, seq_index):
    matches = seq_index[:, None] == jnp.arange(id_table.shape[0], dtype=jnp.int32)[None, :]
    return jnp.sum(jnp.where(matches, id_table[None, :], 0), axis=1)


def keep_factor(
    token_index, column_index, example_ids, sample_ids, layer_index, dropout_seed, stream_tag
):
    seq_index = token_index // WIN
    position = token_index % WIN + (CTX - WIN)
    row_bits = mix_bits(dropout_seed[1] ^ position)
    row_bits = mix_bits(row_bits ^ layer_index[0] * 2 + stream_tag)
    row_bits = mix_bits(row_bits ^ pick_rows(sample_ids, seq_index))
    row_bits = mix_bits(row_bits ^ pick_rows(example_ids, seq_index))
    row_bits = mix_bits(row_bits ^ dropout_seed[0])
    cell_bits = mix_bits(row_bits[:, None] ^ column_index[None, :] * 1640531527)
    return jnp.where(cell_bits & 65535 >= drop_cut, keep_scale, 0.0).astype(f32)


def shift(value, axis, step):
    n = lax.axis_size(axis)
    return lax.ppermute(value, axis, [(i, (i + step) % n) for i in range(n)])


def spread(value, axis):
    n = lax.axis_size(axis)
    return lax.all_to_all(
        jnp.broadcast_to(value[None], (n,) + value.shape), axis, 0, 0, tiled=True
    )


def together(*values):
    return lax.optimization_barrier(values)


def pair_swap(rows, core):
    kept = lax.dynamic_index_in_dim(rows, core, 0, keepdims=False)
    given = lax.dynamic_index_in_dim(rows, 1 - core, 0, keepdims=False)
    got = shift(given, "c", 1)
    first = core == 0
    return jnp.stack([jnp.where(first, kept, got), jnp.where(first, got, kept)])


def on_device(
    residual,
    queries,
    key_cache,
    value_cache,
    out_proj,
    norm_gain,
    gate_proj,
    up_proj,
    down_proj,
    example_ids,
    sample_ids,
    layer_index,
    dropout_seed,
):
    zl, x, y, zh, c = (lax.axis_index(a) for a in AXES)
    nx, nz, ny = lax.axis_size("x"), lax.axis_size("zl"), lax.axis_size("y")
    quarter = gate_proj.shape[1] // nx
    own_rows, width = residual.shape
    side = width // 2
    away = (2, 1, 3)

    def pick(value, at):
        return lax.dynamic_index_in_dim(value, at, 0, keepdims=False)

    local_ctx = key_cache.shape[1]

    def by_owner(cache):
        return cache.reshape(2, local_ctx, KV_HEADS, HEAD_DIM).transpose(2, 0, 1, 3)

    cache_send = jnp.stack([by_owner(key_cache), by_owner(value_cache)], axis=2)
    cache_send = cache_send.reshape(2 * KV_HEADS, 2, local_ctx, HEAD_DIM)
    cache_got = lax.all_to_all(cache_send, NARROW, 0, 0, tiled=True)

    q_seqs = queries.reshape(2, WIN, -1)
    q_other = shift(pick(q_seqs, 1 - c), "c", 1)
    q_all = jnp.concatenate([pick(q_seqs, c), q_other], axis=1).reshape(WIN * GROUP, HEAD_DIM)
    out_other = shift(out_proj, "c", 1)
    gains = [norm_gain] + [shift(norm_gain, "x", k) for k in range(1, nx)]
    residual_own = pair_swap(residual.reshape(2, WIN, width), c).reshape(own_rows, width)

    def gate_up_piece(k):
        at = (x + k) % nx * quarter
        return jnp.concatenate(
            [
                lax.dynamic_slice_in_dim(gate_proj, at, quarter, 1),
                lax.dynamic_slice_in_dim(up_proj, at, quarter, 1),
            ],
            axis=1,
        )

    def down_piece(k):
        return lax.dynamic_slice_in_dim(down_proj, (x + k) % nx * quarter, quarter, 0)

    pieces = [gate_up_piece(k) for k in range(nx)]
    cache_got, q_all, out_other, residual_own, gains, pieces = together(
        cache_got, q_all, out_other, residual_own, gains, pieces
    )

    keys = cache_got[:, 0].reshape(CTX, HEAD_DIM)
    values = cache_got[:, 1].reshape(CTX, HEAD_DIM)
    scores = lax.dot_general(
        q_all, keys, (((1,), (1,)), ((), ())), preferred_element_type=f32
    ) * (1.0 / math.sqrt(HEAD_DIM))
    row_position = CTX - WIN + jnp.arange(WIN * GROUP, dtype=jnp.int32) // GROUP
    visible = jnp.arange(CTX, dtype=jnp.int32)[None, :] <= row_position[:, None]
    masked = jnp.where(visible, scores, neg_fill)
    weights = jnp.where(visible, jnp.exp(masked - jnp.max(masked, axis=1, keepdims=True)), 0.0)
    totals = jnp.sum(weights, axis=1, keepdims=True)
    attended = jnp.dot(weights.astype(bf16), values, preferred_element_type=f32) / totals
    attended = attended.astype(bf16).reshape(WIN, GROUP * HEAD_DIM)

    att, residual_own, pieces = together(
        spread(spread(attended, "zl"), "x"), residual_own, pieces
    )
    residual_far = shift(residual_own, "zh", 1)
    att = att.transpose(1, 0, 2, 3).reshape(-1, GROUP * HEAD_DIM)

    half = out_proj.shape[0]
    attn_terms = jnp.dot(att[:, :half], out_proj, preferred_element_type=f32) + jnp.dot(
        att[:, half:], out_other, preferred_element_type=f32
    )
    attn_terms = attn_terms.astype(bf16).reshape(ny, 2 * own_rows, width)
    share = pick(attn_terms, y).astype(f32)
    for k in away:
        share = share + shift(pick(attn_terms, (y + k) % ny), "y", k).astype(f32)
    near_pieces = [shift(pieces[1], "x", 1), shift(pieces[3], "x", 3)]
    share, near_pieces, piece_two, residual_far = together(
        share.astype(bf16), near_pieces, pieces[2], residual_far
    )
    share_other = shift(share, "zh", 1)
    top = shift(piece_two[:side], "x", 2)
    share_other, top, piece_two = together(share_other, top, piece_two)
    low = shift(piece_two[side:], "x", 2)
    share = share.astype(f32) + share_other.astype(f32)
    share = share.reshape(2, own_rows, width)
    share = jnp.stack([pick(share, 1 - zh), pick(share, zh)])

    column_index = (zl * nx + x) * width + jnp.arange(width, dtype=jnp.int32)
    row = jnp.arange(own_rows, dtype=jnp.int32)

    def keep_of(half_index, tag):
        chip = 2 * y + half_index
        tokens = (4 * chip + c + 2 * (row // WIN)) * WIN + row % WIN
        return keep_factor(
            tokens, column_index, example_ids, sample_ids, layer_index, dropout_seed, tag
        )

    keep_first = jnp.stack([keep_of(1 - zh, 0), keep_of(zh, 0)])
    residual_both = jnp.stack([residual_far, residual_own])
    stream = (residual_both.astype(f32) + keep_first * share).astype(bf16)

    rows_y = [stream] + [shift(stream, "y", k) for k in range(1, ny)]
    rows_y, low = together(rows_y, low)
    rows_far = jnp.concatenate([r[0] for r in rows_y], axis=0)
    rows_near = jnp.concatenate([r[1] for r in rows_y], axis=0)
    gate_up_own = [pieces[0], near_pieces[0], jnp.concatenate([top, low], axis=0), near_pieces[1]]
    gate_up_pair = [shift(w, "c", 1) for w in gate_up_own]

    def all_columns(rows):
        return [rows] + [shift(rows, "x", k) for k in range(1, nx)]

    def gate_up_terms(blocks):
        squares = own = pair = 0.0
        for block, g, w, v in zip(blocks, gains, gate_up_own, gate_up_pair):
            block = block.astype(f32)
            squares = squares + jnp.sum(jnp.square(block), axis=1, keepdims=True)
            block = (block * g.astype(f32)[None, :]).astype(bf16)
            own = own + jnp.dot(block, w, preferred_element_type=f32)
            pair = pair + jnp.dot(block, v, preferred_element_type=f32)
        high = lax.reduce_precision(squares, 8, 7)
        middle = lax.reduce_precision(squares - high, 8, 7)
        last = squares - high - middle
        lane = jnp.arange(128, dtype=jnp.int32)[None, :]
        parts = jnp.where(lane == 0, high, jnp.where(lane == 1, middle, last))
        parts = jnp.where(lane < 3, parts, 0.0).astype(bf16)
        sends = jnp.concatenate([own.astype(bf16), pair.astype(bf16), parts], axis=1)
        return sends.reshape(ny, own_rows, -1)

    def sum_rows(sends):
        total = 0.0
        for k in (*away, 0):
            term = pick(sends, (y - zl - k) % ny)
            total = total + (shift(term, "zl", k) if k else term).astype(f32)
        return total

    def gated_units(total):
        squares = jnp.sum(total[:, 4 * quarter :], axis=1, keepdims=True)
        both = total[:, : 4 * quarter] * lax.rsqrt(squares / MODEL_WIDTH + epsilon)
        units = [
            jax.nn.silu(both[:, s * quarter : (s + 1) * quarter])
            * both[:, (s + 1) * quarter : (s + 2) * quarter]
            for s in (0, 2)
        ]
        return jnp.concatenate(units, axis=1).astype(bf16)

    def all_rows(hidden):
        return jnp.concatenate([hidden] + [shift(hidden, "zl", k) for k in range(1, nz)], axis=0)

    def sum_columns(hidden):
        terms = 0.0
        for k in (*away, 0):
            term = jnp.dot(hidden[:, :quarter], down_own[k], preferred_element_type=f32)
            term = term + jnp.dot(hidden[:, quarter:], down_pair[k], preferred_element_type=f32)
            terms = terms + (shift(term.astype(bf16), "x", -k).astype(f32) if k else term)
        return terms.astype(bf16).reshape(nz, own_rows, width)

    def sum_y(terms):
        result = 0.0
        for k in (*away, 0):
            term = pick(terms, (zl - y - k) % ny)
            result = result + (shift(term, "y", k) if k else term).astype(f32)
        return result

    rows_near, blocks_far = together(rows_near, all_columns(rows_far))
    sends_far, blocks_near, down_proj = together(
        gate_up_terms(blocks_far), all_columns(rows_near), down_proj
    )
    down_near = [shift(down_piece(1), "x", 1), shift(down_piece(3), "x", 3)]
    sends_near = gate_up_terms(blocks_near)
    total_far, down_near, down_proj = together(sum_rows(sends_far), down_near, down_proj)
    down_far = shift(down_piece(2), "x", 2)
    hidden_far, total_near, down_far = together(
        all_rows(gated_units(total_far)), sum_rows(sends_near), down_far
    )
    down_own = [down_piece(0), down_near[0], down_far, down_near[1]]
    down_pair = [shift(w, "c", 1) for w in down_own]
    terms_far, hidden_near = together(
        sum_columns(hidden_far), all_rows(gated_units(total_near))
    )
    far, terms_near = together(sum_y(terms_far), sum_columns(hidden_near))
    near = sum_y(terms_near)
    ffn_share = near + shift(far.astype(bf16), "zh", 1).astype(f32)
    layer_out = (stream[1].astype(f32) + keep_of(zh, 1) * ffn_share).astype(bf16)
    return pair_swap(layer_out.reshape(2, WIN, width), c).reshape(own_rows, width)


def solution(mesh):
    fine = Mesh(mesh.devices.reshape(4, 4, 4, 2, 2), AXES)
    return jax.shard_map(
        on_device,
        mesh=fine,
        in_specs=(
            P(NARROW, WIDE),
            P(WIDE, NARROW),
            P(WIDE, NARROW, None),
            P(WIDE, NARROW, None),
            P(NARROW, WIDE),
            P(WIDE),
            P(WIDE, NARROW),
            P(WIDE, NARROW),
            P(NARROW, WIDE),
            P(),
            P(),
            P(),
            P(),
        ),
        out_specs=P(NARROW, WIDE),
        check_vma=False,
    )
```

```python
import math

import jax
import jax.numpy as jnp
from jax import lax
from jax.sharding import Mesh, PartitionSpec as P

MODEL_WIDTH = 8192
KV_HEADS = 8
GROUP = 8
HEAD_DIM = 128
CTX = 1024
WIN = 32
AXES = ("zl", "x", "y", "zh", "c")
WIDE = ("zl", "x")
NARROW = ("y", "zh", "c")

drop_cut = 6554
keep_scale = 1.0 / 0.9
epsilon = 1e-05
neg_fill = -1e30
f32 = jnp.float32
bf16 = jnp.bfloat16


def mix_bits(word_bits):
    word_bits = word_bits ^ lax.shift_right_logical(word_bits, jnp.int32(16))
    word_bits = word_bits * 2146121005
    word_bits = word_bits ^ lax.shift_right_logical(word_bits, jnp.int32(15))
    word_bits = word_bits * 1147971211
    word_bits = word_bits ^ lax.shift_right_logical(word_bits, jnp.int32(16))
    return word_bits


def pick_rows(id_table, seq_index):
    matches = seq_index[:, None] == jnp.arange(id_table.shape[0], dtype=jnp.int32)[None, :]
    return jnp.sum(jnp.where(matches, id_table[None, :], 0), axis=1)


def keep_factor(
    token_index, column_index, example_ids, sample_ids, layer_index, dropout_seed, stream_tag
):
    seq_index = token_index // WIN
    position = token_index % WIN + (CTX - WIN)
    row_bits = mix_bits(dropout_seed[1] ^ position)
    row_bits = mix_bits(row_bits ^ layer_index[0] * 2 + stream_tag)
    row_bits = mix_bits(row_bits ^ pick_rows(sample_ids, seq_index))
    row_bits = mix_bits(row_bits ^ pick_rows(example_ids, seq_index))
    row_bits = mix_bits(row_bits ^ dropout_seed[0])
    cell_bits = mix_bits(row_bits[:, None] ^ column_index[None, :] * 1640531527)
    return jnp.where(cell_bits & 65535 >= drop_cut, keep_scale, 0.0).astype(f32)


def shift(value, axis, step):
    n = lax.axis_size(axis)
    return lax.ppermute(value, axis, [(i, (i + step) % n) for i in range(n)])


def spread(value, axis):
    n = lax.axis_size(axis)
    return lax.all_to_all(
        jnp.broadcast_to(value[None], (n,) + value.shape), axis, 0, 0, tiled=True
    )


def together(*values):
    return lax.optimization_barrier(values)


def pair_swap(rows, core):
    kept = lax.dynamic_index_in_dim(rows, core, 0, keepdims=False)
    given = lax.dynamic_index_in_dim(rows, 1 - core, 0, keepdims=False)
    got = shift(given, "c", 1)
    first = core == 0
    return jnp.stack([jnp.where(first, kept, got), jnp.where(first, got, kept)])


def on_device(
    residual,
    queries,
    key_cache,
    value_cache,
    out_proj,
    norm_gain,
    gate_proj,
    up_proj,
    down_proj,
    example_ids,
    sample_ids,
    layer_index,
    dropout_seed,
):
    zl, x, y, zh, c = (lax.axis_index(a) for a in AXES)
    nx, nz, ny = lax.axis_size("x"), lax.axis_size("zl"), lax.axis_size("y")
    quarter = gate_proj.shape[1] // nx
    own_rows, width = residual.shape
    side = width // 2
    away = (2, 1, 3)

    def pick(value, at):
        return lax.dynamic_index_in_dim(value, at, 0, keepdims=False)

    local_ctx = key_cache.shape[1]

    def by_owner(cache):
        return cache.reshape(2, local_ctx, KV_HEADS, HEAD_DIM).transpose(2, 0, 1, 3)

    cache_send = jnp.stack([by_owner(key_cache), by_owner(value_cache)], axis=2)
    cache_send = cache_send.reshape(2 * KV_HEADS, 2, local_ctx, HEAD_DIM)
    cache_got = lax.all_to_all(cache_send, NARROW, 0, 0, tiled=True)

    q_seqs = queries.reshape(2, WIN, -1)
    q_other = shift(pick(q_seqs, 1 - c), "c", 1)
    q_all = jnp.concatenate([pick(q_seqs, c), q_other], axis=1).reshape(WIN * GROUP, HEAD_DIM)
    out_other = shift(out_proj, "c", 1)
    residual_own = pair_swap(residual.reshape(2, WIN, width), c).reshape(own_rows, width)

    def gate_up_piece(k, rows):
        at = (x + k) % nx * quarter
        return jnp.concatenate(
            [
                lax.dynamic_slice_in_dim(gate_proj[rows], at, quarter, 1),
                lax.dynamic_slice_in_dim(up_proj[rows], at, quarter, 1),
            ],
            axis=1,
        )

    def down_piece(k):
        return lax.dynamic_slice_in_dim(down_proj, (x + k) % nx * quarter, quarter, 0)

    upper, lower = slice(0, side), slice(side, width)
    pieces = [gate_up_piece(0, slice(0, width))]
    pieces += [[gate_up_piece(k, upper), gate_up_piece(k, lower)] for k in range(1, nx)]
    cache_got, q_all, out_other, residual_own, norm_gain, pieces = together(
        cache_got, q_all, out_other, residual_own, norm_gain, pieces
    )

    keys = cache_got[:, 0].reshape(CTX, HEAD_DIM)
    values = cache_got[:, 1].reshape(CTX, HEAD_DIM)
    scores = lax.dot_general(
        q_all, keys, (((1,), (1,)), ((), ())), preferred_element_type=f32
    ) * (1.0 / math.sqrt(HEAD_DIM))
    row_position = CTX - WIN + jnp.arange(WIN * GROUP, dtype=jnp.int32) // GROUP
    visible = jnp.arange(CTX, dtype=jnp.int32)[None, :] <= row_position[:, None]
    masked = jnp.where(visible, scores, neg_fill)
    weights = jnp.where(visible, jnp.exp(masked - jnp.max(masked, axis=1, keepdims=True)), 0.0)
    totals = jnp.sum(weights, axis=1, keepdims=True)
    attended = jnp.dot(weights.astype(bf16), values, preferred_element_type=f32) / totals
    attended = attended.astype(bf16).reshape(WIN, GROUP * HEAD_DIM)

    upper_one, upper_three = shift(pieces[1][0], "x", 1), shift(pieces[3][0], "x", 3)
    gains = [norm_gain] + [shift(norm_gain, "x", k) for k in range(1, nx)]
    residual_far = shift(residual_own, "zh", 1)
    att, upper_one, upper_three, gains, residual_far = together(
        spread(attended, "zl"), upper_one, upper_three, gains, residual_far
    )

    column_index = (zl * nx + x) * width + jnp.arange(width, dtype=jnp.int32)
    row = jnp.arange(own_rows, dtype=jnp.int32)

    def keep_of(half_index, tag):
        chip = 2 * y + half_index
        tokens = (4 * chip + c + 2 * (row // WIN)) * WIN + row % WIN
        return keep_factor(
            tokens, column_index, example_ids, sample_ids, layer_index, dropout_seed, tag
        )

    keep_first = jnp.stack([keep_of(1 - zh, 0), keep_of(zh, 0)]).astype(bf16) > 0
    keep_second = keep_of(zh, 1).astype(bf16) > 0
    att, pieces, keep_first, keep_second = together(
        spread(att, "x"), pieces, keep_first, keep_second
    )
    att = att.transpose(1, 0, 2, 3).reshape(-1, GROUP * HEAD_DIM)

    half = out_proj.shape[0]
    attn_terms = jnp.dot(att[:, :half], out_proj, preferred_element_type=f32) + jnp.dot(
        att[:, half:], out_other, preferred_element_type=f32
    )
    attn_terms = attn_terms.astype(bf16).reshape(ny, 2 * own_rows, width)
    share = pick(attn_terms, y).astype(f32)
    for k in away:
        share = share + shift(pick(attn_terms, (y + k) % ny), "y", k).astype(f32)
    lower_one, lower_three = shift(pieces[1][1], "x", 1), shift(pieces[3][1], "x", 3)
    share, lower_one, lower_three, pieces = together(
        share.astype(bf16), lower_one, lower_three, pieces
    )
    share_other = shift(share, "zh", 1)
    piece_one = jnp.concatenate([upper_one, lower_one], axis=0)
    piece_three = jnp.concatenate([upper_three, lower_three], axis=0)
    upper_two = shift(pieces[2][0], "x", 2)
    share_other, upper_two, pieces = together(share_other, upper_two, pieces)
    lower_two = shift(pieces[2][1], "x", 2)
    share = share.astype(f32) + share_other.astype(f32)
    share = share.reshape(2, own_rows, width)
    share = jnp.stack([pick(share, 1 - zh), pick(share, zh)])

    residual_both = jnp.stack([residual_far, residual_own])
    stream = (residual_both.astype(f32) + jnp.where(keep_first, keep_scale, 0.0) * share).astype(bf16)

    rows_y = [stream] + [shift(stream, "y", k) for k in range(1, ny)]
    rows_y, lower_two = together(rows_y, lower_two)
    rows_far = jnp.concatenate([r[0] for r in rows_y], axis=0)
    rows_near = jnp.concatenate([r[1] for r in rows_y], axis=0)
    piece_two = jnp.concatenate([upper_two, lower_two], axis=0)
    gate_up_own = [pieces[0], piece_one, piece_two, piece_three]
    gate_up_pair = [shift(w, "c", 1) for w in gate_up_own]

    def all_columns(rows):
        return [rows] + [shift(rows, "x", k) for k in range(1, nx)]

    def gate_up_terms(blocks):
        squares = own = pair = 0.0
        for block, g, w, v in zip(blocks, gains, gate_up_own, gate_up_pair):
            block = block.astype(f32)
            squares = squares + jnp.sum(jnp.square(block), axis=1, keepdims=True)
            block = (block * g.astype(f32)[None, :]).astype(bf16)
            own = own + jnp.dot(block, w, preferred_element_type=f32)
            pair = pair + jnp.dot(block, v, preferred_element_type=f32)
        high = lax.reduce_precision(squares, 8, 7)
        middle = lax.reduce_precision(squares - high, 8, 7)
        last = squares - high - middle
        lane = jnp.arange(128, dtype=jnp.int32)[None, :]
        parts = jnp.where(lane == 0, high, jnp.where(lane == 1, middle, last))
        parts = jnp.where(lane < 3, parts, 0.0).astype(bf16)
        sends = jnp.concatenate([own.astype(bf16), pair.astype(bf16), parts], axis=1)
        return sends.reshape(ny, own_rows, -1)

    def moved_rows(sends, k):
        return shift(pick(sends, (y - zl - k) % ny), "zl", k)

    def sum_rows(sends, first):
        total = first.astype(f32) + pick(sends, (y - zl) % ny).astype(f32)
        for k in (2, 3):
            total = total + moved_rows(sends, k).astype(f32)
        return total

    def gated_units(total):
        squares = jnp.sum(total[:, 4 * quarter :], axis=1, keepdims=True)
        both = total[:, : 4 * quarter] * lax.rsqrt(squares / MODEL_WIDTH + epsilon)
        units = [
            jax.nn.silu(both[:, s * quarter : (s + 1) * quarter])
            * both[:, (s + 1) * quarter : (s + 2) * quarter]
            for s in (0, 2)
        ]
        return jnp.concatenate(units, axis=1).astype(bf16)

    def all_rows(hidden):
        return jnp.concatenate([hidden] + [shift(hidden, "zl", k) for k in range(1, nz)], axis=0)

    def sum_columns(hidden):
        terms = 0.0
        for k in (*away, 0):
            term = jnp.dot(hidden[:, :quarter], down_own[k], preferred_element_type=f32)
            term = term + jnp.dot(hidden[:, quarter:], down_pair[k], preferred_element_type=f32)
            terms = terms + (shift(term.astype(bf16), "x", -k).astype(f32) if k else term)
        return terms.astype(bf16).reshape(nz, own_rows, width)

    def sum_y(terms):
        result = 0.0
        for k in (*away, 0):
            term = pick(terms, (zl - y - k) % ny)
            result = result + (shift(term, "y", k) if k else term).astype(f32)
        return result

    rows_near, blocks_far = together(rows_near, all_columns(rows_far))
    sends_far = gate_up_terms(blocks_far)
    first_far, sends_far, blocks_near, down_proj = together(
        moved_rows(sends_far, 1), sends_far, all_columns(rows_near), down_proj
    )
    down_near = [shift(down_piece(1), "x", 1), shift(down_piece(3), "x", 3)]
    sends_near = gate_up_terms(blocks_near)
    total_far, down_near, down_proj = together(
        sum_rows(sends_far, first_far), down_near, down_proj
    )
    down_here = [down_piece(0), *down_near]
    down_far = shift(down_piece(2), "x", 2)
    hidden_far, total_near, down_far, down_other = together(
        all_rows(gated_units(total_far)),
        sum_rows(sends_near, moved_rows(sends_near, 1)),
        down_far,
        [shift(w, "c", 1) for w in down_here],
    )
    down_own = [down_here[0], down_here[1], down_far, down_here[2]]
    down_pair = [down_other[0], down_other[1], shift(down_far, "c", 1), down_other[2]]
    terms_far, hidden_near = together(
        sum_columns(hidden_far), all_rows(gated_units(total_near))
    )
    far, terms_near = together(sum_y(terms_far), sum_columns(hidden_near))
    near = sum_y(terms_near)
    ffn_share = near + shift(far.astype(bf16), "zh", 1).astype(f32)
    layer_out = (stream[1].astype(f32) + jnp.where(keep_second, keep_scale, 0.0) * ffn_share).astype(bf16)
    return pair_swap(layer_out.reshape(2, WIN, width), c).reshape(own_rows, width)


def solution(mesh):
    fine = Mesh(mesh.devices.reshape(4, 4, 4, 2, 2), AXES)
    return jax.shard_map(
        on_device,
        mesh=fine,
        in_specs=(
            P(NARROW, WIDE),
            P(WIDE, NARROW),
            P(WIDE, NARROW, None),
            P(WIDE, NARROW, None),
            P(NARROW, WIDE),
            P(WIDE),
            P(WIDE, NARROW),
            P(WIDE, NARROW),
            P(NARROW, WIDE),
            P(),
            P(),
            P(),
            P(),
        ),
        out_specs=P(NARROW, WIDE),
        check_vma=False,
    )
```

```python
import math

import jax
import jax.numpy as jnp
from jax import lax
from jax.sharding import Mesh, PartitionSpec as P

MODEL_WIDTH = 8192
KV_HEADS = 8
GROUP = 8
HEAD_DIM = 128
CTX = 1024
WIN = 32
AXES = ("zl", "x", "y", "zh", "c")
WIDE = ("zl", "x")
NARROW = ("y", "zh", "c")

drop_cut = 6554
keep_scale = 1.0 / 0.9
epsilon = 1e-05
neg_fill = -1e30
f32 = jnp.float32
bf16 = jnp.bfloat16


def mix_bits(word_bits):
    word_bits = word_bits ^ lax.shift_right_logical(word_bits, jnp.int32(16))
    word_bits = word_bits * 2146121005
    word_bits = word_bits ^ lax.shift_right_logical(word_bits, jnp.int32(15))
    word_bits = word_bits * 1147971211
    word_bits = word_bits ^ lax.shift_right_logical(word_bits, jnp.int32(16))
    return word_bits


def pick_rows(id_table, seq_index):
    matches = seq_index[:, None] == jnp.arange(id_table.shape[0], dtype=jnp.int32)[None, :]
    return jnp.sum(jnp.where(matches, id_table[None, :], 0), axis=1)


def keep_factor(
    token_index, column_index, example_ids, sample_ids, layer_index, dropout_seed, stream_tag
):
    seq_index = token_index // WIN
    position = token_index % WIN + (CTX - WIN)
    row_bits = mix_bits(dropout_seed[1] ^ position)
    row_bits = mix_bits(row_bits ^ layer_index[0] * 2 + stream_tag)
    row_bits = mix_bits(row_bits ^ pick_rows(sample_ids, seq_index))
    row_bits = mix_bits(row_bits ^ pick_rows(example_ids, seq_index))
    row_bits = mix_bits(row_bits ^ dropout_seed[0])
    cell_bits = mix_bits(row_bits[:, None] ^ column_index[None, :] * 1640531527)
    return jnp.where(cell_bits & 65535 >= drop_cut, keep_scale, 0.0).astype(f32)


def shift(value, axis, step):
    n = lax.axis_size(axis)
    return lax.ppermute(value, axis, [(i, (i + step) % n) for i in range(n)])


def spread(value, axis):
    n = lax.axis_size(axis)
    return lax.all_to_all(
        jnp.broadcast_to(value[None], (n,) + value.shape), axis, 0, 0, tiled=True
    )


def together(*values):
    return lax.optimization_barrier(values)


def pair_swap(rows, core):
    kept = lax.dynamic_index_in_dim(rows, core, 0, keepdims=False)
    given = lax.dynamic_index_in_dim(rows, 1 - core, 0, keepdims=False)
    got = shift(given, "c", 1)
    first = core == 0
    return jnp.stack([jnp.where(first, kept, got), jnp.where(first, got, kept)])


def on_device(
    residual,
    queries,
    key_cache,
    value_cache,
    out_proj,
    norm_gain,
    gate_proj,
    up_proj,
    down_proj,
    example_ids,
    sample_ids,
    layer_index,
    dropout_seed,
):
    zl, x, y, zh, c = (lax.axis_index(a) for a in AXES)
    nx, nz, ny = lax.axis_size("x"), lax.axis_size("zl"), lax.axis_size("y")
    quarter = gate_proj.shape[1] // nx
    own_rows, width = residual.shape
    side = width // 2
    away = (2, 1, 3)

    def pick(value, at):
        return lax.dynamic_index_in_dim(value, at, 0, keepdims=False)

    local_ctx = key_cache.shape[1]

    def by_owner(cache):
        return cache.reshape(2, local_ctx, KV_HEADS, HEAD_DIM).transpose(2, 0, 1, 3)

    cache_send = jnp.stack([by_owner(key_cache), by_owner(value_cache)], axis=2)
    cache_send = cache_send.reshape(2 * KV_HEADS, 2, local_ctx, HEAD_DIM)
    cache_got = lax.all_to_all(cache_send, NARROW, 0, 0, tiled=True)

    q_seqs = queries.reshape(2, WIN, -1)
    q_other = shift(pick(q_seqs, 1 - c), "c", 1)
    q_all = jnp.concatenate([pick(q_seqs, c), q_other], axis=1).reshape(WIN * GROUP, HEAD_DIM)
    out_other = shift(out_proj, "c", 1)
    residual_own = pair_swap(residual.reshape(2, WIN, width), c).reshape(own_rows, width)

    def gate_up_piece(k, rows):
        at = (x + k) % nx * quarter
        return jnp.concatenate(
            [
                lax.dynamic_slice_in_dim(gate_proj[rows], at, quarter, 1),
                lax.dynamic_slice_in_dim(up_proj[rows], at, quarter, 1),
            ],
            axis=1,
        )

    def down_piece(k):
        return lax.dynamic_slice_in_dim(down_proj, (x + k) % nx * quarter, quarter, 0)

    upper, lower = slice(0, side), slice(side, width)
    pieces = [gate_up_piece(0, slice(0, width))]
    pieces += [[gate_up_piece(k, upper), gate_up_piece(k, lower)] for k in range(1, nx)]
    cache_got, q_all, out_other, residual_own, norm_gain, pieces = together(
        cache_got, q_all, out_other, residual_own, norm_gain, pieces
    )

    keys = cache_got[:, 0].reshape(CTX, HEAD_DIM)
    values = cache_got[:, 1].reshape(CTX, HEAD_DIM)
    scores = lax.dot_general(
        q_all, keys, (((1,), (1,)), ((), ())), preferred_element_type=f32
    ) * (1.0 / math.sqrt(HEAD_DIM))
    row_position = CTX - WIN + jnp.arange(WIN * GROUP, dtype=jnp.int32) // GROUP
    visible = jnp.arange(CTX, dtype=jnp.int32)[None, :] <= row_position[:, None]
    masked = jnp.where(visible, scores, neg_fill)
    weights = jnp.where(visible, jnp.exp(masked - jnp.max(masked, axis=1, keepdims=True)), 0.0)
    totals = jnp.sum(weights, axis=1, keepdims=True)
    attended = jnp.dot(weights.astype(bf16), values, preferred_element_type=f32) / totals
    attended = attended.astype(bf16).reshape(WIN, GROUP * HEAD_DIM)

    upper_one, upper_three = shift(pieces[1][0], "x", 1), shift(pieces[3][0], "x", 3)
    att, upper_one, upper_three, norm_gain = together(
        spread(attended, "zl"), upper_one, upper_three, norm_gain
    )
    gains = [norm_gain] + [shift(norm_gain, "x", k) for k in range(1, nx)]

    column_index = (zl * nx + x) * width + jnp.arange(width, dtype=jnp.int32)
    row = jnp.arange(own_rows, dtype=jnp.int32)

    def keep_of(half_index, tag):
        chip = 2 * y + half_index
        tokens = (4 * chip + c + 2 * (row // WIN)) * WIN + row % WIN
        return keep_factor(
            tokens, column_index, example_ids, sample_ids, layer_index, dropout_seed, tag
        )

    keep_first = jnp.stack([keep_of(1 - zh, 0), keep_of(zh, 0)]).astype(bf16) > 0
    keep_second = keep_of(zh, 1).astype(bf16) > 0
    att, pieces, keep_first, keep_second, gains = together(
        spread(att, "x"), pieces, keep_first, keep_second, gains
    )
    att = att.transpose(1, 0, 2, 3).reshape(-1, GROUP * HEAD_DIM)

    half = out_proj.shape[0]
    attn_terms = jnp.dot(att[:, :half], out_proj, preferred_element_type=f32) + jnp.dot(
        att[:, half:], out_other, preferred_element_type=f32
    )
    attn_terms = attn_terms.astype(bf16).reshape(ny, 2 * own_rows, width)
    share = pick(attn_terms, y).astype(f32)
    for k in away:
        share = share + shift(pick(attn_terms, (y + k) % ny), "y", k).astype(f32)
    lower_one, lower_three = shift(pieces[1][1], "x", 1), shift(pieces[3][1], "x", 3)
    share, lower_one, lower_three, pieces = together(
        share.astype(bf16), lower_one, lower_three, pieces
    )
    share = share.reshape(2, own_rows, width)
    share_other = shift(jnp.concatenate([share, residual_own[None]], axis=0), "zh", 1)
    piece_one = jnp.concatenate([upper_one, lower_one], axis=0)
    piece_three = jnp.concatenate([upper_three, lower_three], axis=0)
    upper_two = shift(pieces[2][0], "x", 2)
    share_other, upper_two, pieces = together(share_other, upper_two, pieces)
    lower_two = shift(pieces[2][1], "x", 2)
    residual_far = share_other[2]
    share = share.astype(f32) + share_other[:2].astype(f32)
    share = jnp.stack([pick(share, 1 - zh), pick(share, zh)])

    residual_both = jnp.stack([residual_far, residual_own])
    stream = (residual_both.astype(f32) + jnp.where(keep_first, keep_scale, 0.0) * share).astype(bf16)

    rows_y = [stream] + [shift(stream, "y", k) for k in range(1, ny)]
    rows_y, lower_two = together(rows_y, lower_two)
    rows_far = jnp.concatenate([r[0] for r in rows_y], axis=0)
    rows_near = jnp.concatenate([r[1] for r in rows_y], axis=0)
    piece_two = jnp.concatenate([upper_two, lower_two], axis=0)
    gate_up_own = [pieces[0], piece_one, piece_two, piece_three]
    gate_up_pair = [shift(w, "c", 1) for w in gate_up_own]

    def all_columns(rows):
        return [rows] + [shift(rows, "x", k) for k in range(1, nx)]

    def gate_up_terms(blocks):
        squares = own = pair = 0.0
        for block, g, w, v in zip(blocks, gains, gate_up_own, gate_up_pair):
            block = block.astype(f32)
            squares = squares + jnp.sum(jnp.square(block), axis=1, keepdims=True)
            block = (block * g.astype(f32)[None, :]).astype(bf16)
            own = own + jnp.dot(block, w, preferred_element_type=f32)
            pair = pair + jnp.dot(block, v, preferred_element_type=f32)
        high = lax.reduce_precision(squares, 8, 7)
        middle = lax.reduce_precision(squares - high, 8, 7)
        last = squares - high - middle
        lane = jnp.arange(128, dtype=jnp.int32)[None, :]
        parts = jnp.where(lane == 0, high, jnp.where(lane == 1, middle, last))
        parts = jnp.where(lane < 3, parts, 0.0).astype(bf16)
        sends = jnp.concatenate([own.astype(bf16), pair.astype(bf16), parts], axis=1)
        return sends.reshape(ny, own_rows, -1)

    def moved_rows(sends, k):
        return shift(pick(sends, (y - zl - k) % ny), "zl", k)

    def sum_rows(sends, first):
        total = first.astype(f32) + pick(sends, (y - zl) % ny).astype(f32)
        for k in (2, 3):
            total = total + moved_rows(sends, k).astype(f32)
        return total

    def gated_units(total):
        squares = jnp.sum(total[:, 4 * quarter :], axis=1, keepdims=True)
        both = total[:, : 4 * quarter] * lax.rsqrt(squares / MODEL_WIDTH + epsilon)
        units = [
            jax.nn.silu(both[:, s * quarter : (s + 1) * quarter])
            * both[:, (s + 1) * quarter : (s + 2) * quarter]
            for s in (0, 2)
        ]
        return jnp.concatenate(units, axis=1).astype(bf16)

    def all_rows(hidden):
        return jnp.concatenate([hidden] + [shift(hidden, "zl", k) for k in range(1, nz)], axis=0)

    def sum_columns(hidden):
        terms = 0.0
        for k in (*away, 0):
            term = jnp.dot(hidden[:, :quarter], down_own[k], preferred_element_type=f32)
            term = term + jnp.dot(hidden[:, quarter:], down_pair[k], preferred_element_type=f32)
            terms = terms + (shift(term.astype(bf16), "x", -k).astype(f32) if k else term)
        return terms.astype(bf16).reshape(nz, own_rows, width)

    def sum_y(terms):
        result = 0.0
        for k in (*away, 0):
            term = pick(terms, (zl - y - k) % ny)
            result = result + (shift(term, "y", k) if k else term).astype(f32)
        return result

    rows_near, blocks_far = together(rows_near, all_columns(rows_far))
    sends_far = gate_up_terms(blocks_far)
    first_far, sends_far, blocks_near, down_proj = together(
        moved_rows(sends_far, 1), sends_far, all_columns(rows_near), down_proj
    )
    down_near = [shift(down_piece(1), "x", 1), shift(down_piece(3), "x", 3)]
    sends_near = gate_up_terms(blocks_near)
    total_far, down_near, down_proj = together(
        sum_rows(sends_far, first_far), down_near, down_proj
    )
    down_here = [down_piece(0), *down_near]
    down_far = shift(down_piece(2), "x", 2)
    hidden_far, total_near, down_far, down_other = together(
        all_rows(gated_units(total_far)),
        sum_rows(sends_near, moved_rows(sends_near, 1)),
        down_far,
        [shift(w, "c", 1) for w in down_here],
    )
    down_own = [down_here[0], down_here[1], down_far, down_here[2]]
    down_pair = [down_other[0], down_other[1], shift(down_far, "c", 1), down_other[2]]
    terms_far, hidden_near = together(
        sum_columns(hidden_far), all_rows(gated_units(total_near))
    )
    far, terms_near = together(sum_y(terms_far), sum_columns(hidden_near))
    near = sum_y(terms_near)
    ffn_share = near + shift(far.astype(bf16), "zh", 1).astype(f32)
    layer_out = (stream[1].astype(f32) + jnp.where(keep_second, keep_scale, 0.0) * ffn_share).astype(bf16)
    return pair_swap(layer_out.reshape(2, WIN, width), c).reshape(own_rows, width)


def solution(mesh):
    fine = Mesh(mesh.devices.reshape(4, 4, 4, 2, 2), AXES)
    return jax.shard_map(
        on_device,
        mesh=fine,
        in_specs=(
            P(NARROW, WIDE),
            P(WIDE, NARROW),
            P(WIDE, NARROW, None),
            P(WIDE, NARROW, None),
            P(NARROW, WIDE),
            P(WIDE),
            P(WIDE, NARROW),
            P(WIDE, NARROW),
            P(NARROW, WIDE),
            P(),
            P(),
            P(),
            P(),
        ),
        out_specs=P(NARROW, WIDE),
        check_vma=False,
    )
```
